32 devices in a mesh: grp: 2 (over y), ch: 4 (over z), tm: 2 (over x), sub: 2 (over core).
Axes of the slice: x: 2, y: 2, z: 4, core: 2. Of those that a mesh axis runs over, the one named last changes fastest.
Arguments:
- record: bfloat16 [256, 1024], P(('grp', 'ch'), ('tm', 'sub')), parts along dimension 0, may hold values from -8 to 8
- freq_bins: int32 [64], P('grp'), parts along dimension 0, may hold values from 1 to 511, as said below
- wave_limit: int32 [64], P('grp'), parts along dimension 0, may hold values from 1 to 64
- pick_index: int32 [128], P(('grp', 'ch')), parts along dimension 0, may hold values from 0 to 1023
- weight_first: bfloat16 [9, 32], replicated, may hold values from -2 to 2
- weight_second: bfloat16 [9, 32, 32], replicated, may hold values from -0.375 to 0.375
- weight_stride: bfloat16 [4, 64, 32], replicated, may hold values from -0.5 to 0.5
- weight_third: bfloat16 [9, 64, 64], replicated, may hold values from -0.25 to 0.25
- weight_head: bfloat16 [64], replicated, may hold values from -0.75 to 0.75
Outputs:
- filtered: bfloat16 [256, 1024], P(('grp', 'ch'), ('tm', 'sub')), parts along dimension 0
- logits: float32 [128, 512], P(('grp', 'ch'), ('tm', 'sub')), parts along dimension 0
- filtered_grad: float32 [256, 1024], P(('grp', 'ch'), ('tm', 'sub')), parts along dimension 0
The draws below stay inside these ranges and needn't reach their ends.
There are 2 independent parts, one for each index of `grp`. The reference program is written for one: setup_inputs(seed, part) draws one part's arguments, and reference() takes and returns one part's arrays. A program takes and returns all parts, laid end to end along the dimension named above; an argument that names none is the same for every part. Nothing has to cross between parts.
Inputs may be any that keep to these rules, and one draw needn't show every extreme that they name: `freq_bins`: distinct bins, none of them 0 or 512.
All inputs are finite; a program needn't handle non-finite values.
Results may differ from the reference program's by a relative error of at most 0.02.
Values may be sent and summed in bfloat16 or wider, within the bound.
A program may use at most 64 MiB of HBM per device.

```python
import jax
import jax.numpy as jnp
from jax import lax

F1 = 32
F2 = 64
SIGMA = 64
CHANNELS = 128
SAMPLES = 1024
FREQS = 32
COARSE_CH = 64
COARSE_T = 512


def draw_record(key, part):
    key_base, key_row = jax.random.split(key)
    position = jnp.arange(CHANNELS, dtype=jnp.int32).astype(jnp.float32) / CHANNELS
    jitter = jnp.exp(jax.random.uniform(key_row, (CHANNELS, 1), jnp.float32, -0.69, 0.69))
    baseline = jnp.clip(jax.random.normal(key_base, (CHANNELS, SAMPLES), jnp.float32), -4.0, 4.0) * 0.25
    growth = jnp.power(3.0, 1.0 - position)
    return (baseline * growth[:, None] * jitter).astype(jnp.bfloat16)


def draw_freq_bins(key, part):
    shuffled = jax.random.permutation(key, SAMPLES // 2 - 1)
    return (shuffled[:FREQS] + 1).astype(jnp.int32)


def plant(array, rng, smallest, high):
    index_at = [jax.random.randint(jax.random.fold_in(rng, axis), (), 0, length) for axis, length in enumerate(array.shape)]
    widest = array.shape.index(max(array.shape))
    beside = index_at[:widest] + [(index_at[widest] + 1) % array.shape[widest]] + index_at[widest + 1:]
    return array.at[tuple(index_at)].set(smallest).at[tuple(beside)].set(high)


def centred(key, shape, width, reach, kind=jnp.bfloat16):
    drawn = jax.random.normal(key, shape, jnp.float32) * width
    return jnp.minimum(jnp.maximum(drawn, -reach), reach).astype(kind)


def setup_inputs(seed: int = 0, part: int = 0) -> dict:
    keys = jax.random.split(jax.random.key(seed), 10)
    own_keys = jax.random.split(jax.random.fold_in(keys[9], part), 10)
    record = draw_record(jax.random.fold_in(jax.random.fold_in(keys[9], part), 71), part)
    freq_bins = draw_freq_bins(jax.random.fold_in(jax.random.fold_in(keys[9], part), 71), part)
    wave_limit = plant(jax.random.randint(own_keys[2], (FREQS,), 1, CHANNELS // 2 + 1), jax.random.fold_in(own_keys[2], 1), 1, (CHANNELS // 2 + 1) - 1).astype(jnp.int32)
    pick_index = plant(jax.random.randint(own_keys[3], (COARSE_CH,), 0, SAMPLES), jax.random.fold_in(own_keys[3], 1), 0, SAMPLES - 1).astype(jnp.int32)
    weight_first = centred(keys[4], (9, F1), 9 ** -0.5, 2.0)
    weight_second = centred(keys[5], (9, F1, F1), (9 * F1) ** -0.5, 0.375)
    weight_stride = centred(keys[6], (4, F2, F1), (4 * F1) ** -0.5, 0.5)
    weight_third = centred(keys[7], (9, F2, F2), (9 * F2) ** -0.5, 0.25)
    weight_head = centred(keys[8], (F2,), F2 ** -0.5, 0.75)
    return dict(record=record, freq_bins=freq_bins, wave_limit=wave_limit, pick_index=pick_index, weight_first=weight_first, weight_second=weight_second, weight_stride=weight_stride, weight_third=weight_third, weight_head=weight_head)


def silu_slope(preact):
    sigma_part = jax.nn.sigmoid(preact)
    return sigma_part * (1.0 + preact * (1.0 - sigma_part))


def silu_round(preact):
    return (preact * jax.nn.sigmoid(preact)).astype(jnp.bfloat16)


def pad_edges(values):
    return jnp.pad(values, ((0, 0), (1, 1), (1, 1)))


def conv_forward(padded, weight, height, breadth):
    summed_up = None
    for kernel_tap in range(9):
        shift_row, shift_col = kernel_tap // 3, kernel_tap % 3
        window = padded[:, shift_row:shift_row + height, shift_col:shift_col + breadth].astype(jnp.float32)
        addend = jnp.einsum('oi,ihw->ohw', weight[kernel_tap].astype(jnp.float32), window)
        summed_up = addend if summed_up is None else summed_up + addend
    return summed_up


def conv_backward(padded_grad, weight, height, breadth):
    summed_up = None
    for kernel_tap in range(9):
        shift_row, shift_col = kernel_tap // 3, kernel_tap % 3
        window = padded_grad[:, 2 - shift_row:2 - shift_row + height, 2 - shift_col:2 - shift_col + breadth].astype(jnp.float32)
        addend = jnp.einsum('oi,ohw->ihw', weight[kernel_tap].astype(jnp.float32), window)
        summed_up = addend if summed_up is None else summed_up + addend
    return summed_up


def reference(record, freq_bins, wave_limit, pick_index, weight_first, weight_second, weight_stride, weight_third, weight_head):
    signal = record.astype(jnp.float32)
    onesided = jnp.fft.rfft(signal, axis=1)[:, freq_bins]
    spectrum_real = jnp.real(onesided).astype(jnp.bfloat16)
    spectrum_imag = jnp.imag(onesided).astype(jnp.bfloat16)
    spectrum_real, spectrum_imag = lax.optimization_barrier((spectrum_real, spectrum_imag))
    spectrum = spectrum_real.astype(jnp.float32) + 1j * spectrum_imag.astype(jnp.float32)
    wave_spec = jnp.fft.fft(spectrum, axis=0)
    wave_index = jnp.arange(CHANNELS, dtype=jnp.int32)
    wave_abs = jnp.minimum(wave_index, CHANNELS - wave_index)
    passing = (wave_abs[:, None] <= wave_limit[None, :]).astype(jnp.float32)
    passed = jnp.fft.ifft(wave_spec * passing, axis=0)
    passband_real = jnp.real(passed).astype(jnp.bfloat16)
    passband_imag = jnp.imag(passed).astype(jnp.bfloat16)
    passband_real, passband_imag = lax.optimization_barrier((passband_real, passband_imag))
    passband = passband_real.astype(jnp.float32) + 1j * passband_imag.astype(jnp.float32)
    onesided_full = jnp.zeros((CHANNELS, SAMPLES // 2 + 1), dtype=passband.dtype)
    onesided_full = onesided_full.at[:, freq_bins].set(passband)
    filtered = jnp.fft.irfft(onesided_full, n=SAMPLES, axis=1).astype(jnp.bfloat16)

    weight_first_full = weight_first[:, :, None]
    padded_input = pad_edges(filtered[None])
    pre_first = conv_forward(padded_input, weight_first_full, CHANNELS, SAMPLES)
    act_first = silu_round(pre_first)
    padded_first = pad_edges(act_first)
    pre_second = conv_forward(padded_first, weight_second, CHANNELS, SAMPLES)
    act_second = silu_round(pre_second)
    pre_stride = None
    for kernel_tap in range(4):
        shift_row, shift_col = kernel_tap // 2, kernel_tap % 2
        window = act_second[:, shift_row::2, shift_col::2].astype(jnp.float32)
        addend = jnp.einsum('oi,ihw->ohw', weight_stride[kernel_tap].astype(jnp.float32), window)
        pre_stride = addend if pre_stride is None else pre_stride + addend
    act_stride = silu_round(pre_stride)
    padded_stride = pad_edges(act_stride)
    pre_third = conv_forward(padded_stride, weight_third, COARSE_CH, COARSE_T)
    act_third = silu_round(pre_third)
    act_wide = act_third.astype(jnp.float32)
    head_wide = weight_head.astype(jnp.float32)
    logits = jnp.einsum('o,ohw->hw', head_wide, act_wide)

    coarse_time = 2.0 * jnp.arange(COARSE_T, dtype=jnp.int32).astype(jnp.float32)
    offsets = (coarse_time[None, :] - pick_index[:, None].astype(jnp.float32)) / SIGMA
    target = jnp.exp(-0.5 * offsets * offsets)
    slope_out = jax.nn.sigmoid(logits) - target

    delta_third = (head_wide[:, None, None] * slope_out[None] * silu_slope(pre_third)).astype(jnp.bfloat16)
    back_stride = conv_backward(pad_edges(delta_third), weight_third, COARSE_CH, COARSE_T)
    delta_stride = (back_stride * silu_slope(pre_stride)).astype(jnp.bfloat16)
    delta_wide = delta_stride.astype(jnp.float32)
    pieces = []
    for kernel_tap in range(4):
        pieces.append(jnp.einsum('oi,ohw->ihw', weight_stride[kernel_tap].astype(jnp.float32), delta_wide))
    regrid = jnp.stack([jnp.stack([pieces[0], pieces[1]], axis=-1), jnp.stack([pieces[2], pieces[3]], axis=-1)], axis=2)
    back_second = regrid.reshape(F1, CHANNELS, SAMPLES)
    delta_second = (back_second * silu_slope(pre_second)).astype(jnp.bfloat16)
    back_first = conv_backward(pad_edges(delta_second), weight_second, CHANNELS, SAMPLES)
    delta_first = (back_first * silu_slope(pre_first)).astype(jnp.bfloat16)
    filtered_grad = conv_backward(pad_edges(delta_first), weight_first_full, CHANNELS, SAMPLES)[0]
    return filtered, logits, filtered_grad
```

```python
import functools
import math

import jax
import jax.numpy as jnp
from jax import lax
from jax.experimental import pallas as pl
from jax.experimental.pallas import tpu as pltpu
from jax.sharding import PartitionSpec as P

SIGMA = 64
HALO = 4
MARGIN = 256
F32 = jnp.float32
BF16 = jnp.bfloat16
SHIFTS = [(sy, sx) for sy in (-1, 0, 1) for sx in (-1, 0, 1)]
PATCH = [(y, x) for y in (-1, 0, 1, 2) for x in (-1, 0, 1, 2)]


def mm(lhs, rhs):
    return jnp.dot(lhs, rhs, preferred_element_type=F32)


def mm_nt(lhs, rhs):
    return lax.dot_general(lhs, rhs, (((1,), (1,)), ((), ())), preferred_element_type=F32)


def split(value):
    high = value.astype(BF16)
    return high, (value - high.astype(F32)).astype(BF16)


def cosine_turns(count, samples):
    folded = jnp.abs(count - samples // 2).astype(F32)
    z = folded * (2.0 * math.pi / samples) - (math.pi / 2)
    z2 = z * z
    poly = jnp.full_like(z2, -1.0 / 39916800)
    for term in (362880, -5040, 120, -6, 1):
        poly = poly * z2 + 1.0 / term
    return z * poly


def table(freq_row, freqs, first_time, step, length, samples):
    time = first_time + step * lax.broadcasted_iota(jnp.int32, (length, 2 * freqs), 0)
    lane = lax.broadcasted_iota(jnp.int32, (length, 2 * freqs), 1)
    quarter = jnp.where(lane >= freqs, samples // 4, 0)
    return cosine_turns((freq_row * time + quarter) & (samples - 1), samples)


def silu_parts(v):
    s = 0.5 * jnp.tanh(0.5 * v) + 0.5
    y = v * s
    return y, s + y * (1.0 - s)


class Geometry:
    def __init__(self, rows, cols):
        self.rows, self.cols = rows, cols
        self.high = rows + 2 * HALO
        self.pitch = cols + 2 * HALO
        self.size = self.high * self.pitch
        self.padded = -(-self.size // 256) * 256
        self.width = self.padded + 2 * MARGIN
        count = 2
        tiles = self.padded // 128
        self.chunks = []
        at = 0
        for i in range(count):
            end = tiles * (i + 1) // count
            self.chunks.append((at * 128, (end - at) * 128))
            at = end

    def offset(self, sy, sx):
        return sy * self.pitch + sx


def unet(geo, samples, total_rows, pb, freq_row, freqs, pick_col, me_ch, me_t, refs, outs, scr):
    w1_ref, w2_ref, ws_ref, w3_ref, wh_ref = refs
    filt_o, logit_o, grad_o = outs
    x0, mask_s, targ_s, act1, sl1, sl2, act_s, sls, dl3, dl2, zs, log_s, grad_s, un = scr
    rows, cols, pitch = geo.rows, geo.cols, geo.pitch
    total_cols = samples // 2
    scale = 2.0 / samples
    f1 = w2_ref.shape[1]
    for ref in (x0, act1, act_s, dl3, dl2, zs):
        n = ref.shape[0]
        ref[:, :MARGIN] = jnp.zeros((n, MARGIN), ref.dtype)
        ref[:, MARGIN + geo.padded :] = jnp.zeros((n, MARGIN), ref.dtype)
    place = lax.broadcasted_iota(jnp.int32, (8, geo.padded), 1).astype(F32)[:1]
    row = jnp.floor((place + 0.5) * (1.0 / pitch))
    col = place - row * pitch
    grow = row + (me_ch * rows - HALO).astype(F32)
    gcol = col + (me_t * cols - HALO).astype(F32)
    inside = (grow >= 0) & (grow < total_rows) & (gcol >= 0) & (gcol < total_cols) & (row < geo.high)
    mask = jnp.where(inside, 1.0, 0.0)
    mask_s[...] = jnp.broadcast_to(mask, mask_s.shape)
    rid = lax.broadcasted_iota(jnp.int32, (geo.high, geo.padded), 0).astype(F32)
    pick = jnp.sum(jnp.where(rid == row, pick_col, 0.0), axis=0, keepdims=True)
    offs = (2.0 * gcol - pick) * (1.0 / SIGMA)
    targ_s[...] = jnp.broadcast_to(jnp.exp(-0.5 * offs * offs), targ_s.shape)
    w2 = [w2_ref[k].astype(F32) for k in range(9)]
    zero = jnp.zeros_like(w2[0])

    def tap(y, x, a, b, sign):
        ky, kx = sign * (y - a) + 1, sign * (x - b) + 1
        return w2[3 * ky + kx] if 0 <= ky < 3 and 0 <= kx < 3 else zero

    phases = [(a, b) for a in (0, 1) for b in (0, 1)]
    w2_f = jnp.concatenate(
        [jnp.concatenate([tap(y, x, a, b, 1) for y, x in PATCH], axis=1) for a, b in phases], axis=0
    ).astype(BF16)
    w2_b = jnp.concatenate(
        [jnp.concatenate([tap(y, x, a, b, -1) for a, b in phases], axis=1) for y, x in PATCH], axis=0
    ).T.astype(BF16)
    ws_f32 = jnp.concatenate([ws_ref[k].astype(F32) for k in range(4)], axis=1)
    ws_f, ws_b = ws_f32.astype(BF16), ws_f32.T.astype(BF16)
    w3 = [w3_ref[k].astype(F32) for k in range(9)]
    w3_f = jnp.concatenate(w3, axis=1).astype(BF16)
    w3_b = jnp.concatenate(w3, axis=0).T.astype(BF16)
    head = jnp.broadcast_to(wh_ref[...].astype(F32), (8, wh_ref.shape[1]))
    head_col = head.T[:, :1]
    head_row = head.astype(BF16)
    srow = lax.broadcasted_iota(jnp.int32, (72, 9), 0)
    tapi = lax.broadcasted_iota(jnp.int32, (72, 9), 1)
    w1 = w1_ref[...]
    parts = []
    for a, b in phases:
        sel = jnp.zeros((72, 9), F32)
        for s, (sy, sx) in enumerate(SHIFTS):
            for p, (py, px) in enumerate(phases):
                ky, kx = 2 * sy + py - a + 1, 2 * sx + px - b + 1
                if 0 <= ky < 3 and 0 <= kx < 3:
                    sel = jnp.where((srow == 8 * s + p) & (tapi == 3 * ky + kx), 1.0, sel)
        parts.append(mm(sel.astype(BF16), w1))
    w1_b32 = jnp.concatenate(parts, axis=1)
    w1_f, w1_b = w1_b32.T.astype(BF16), w1_b32.astype(BF16)

    nat_h, nat_l = split(table(freq_row, freqs, me_t * 2 * cols, 1, 2 * cols, samples))
    nat = (mm_nt(pb, nat_h) + mm_nt(pb, nat_l)) * scale
    filt_o[...] = nat[2 * HALO : 2 * HALO + 2 * rows].astype(BF16)
    x0[...] = jnp.zeros_like(x0)
    for b in range(2):
        t_h, t_l = split(
            table(freq_row, freqs, me_t * 2 * cols - 2 * HALO + b, 2, geo.pitch, samples)
        )
        un[:, :pitch] = (mm_nt(pb, t_h) + mm_nt(pb, t_l)) * scale
        for r in range(geo.high):
            at = MARGIN + r * pitch
            for a in range(2):
                x0[2 * a + b : 2 * a + b + 1, at : at + pitch] = un[2 * r + a : 2 * r + a + 1, :pitch]
    x0[:, MARGIN : MARGIN + geo.padded] = x0[:, MARGIN : MARGIN + geo.padded] * mask_s[...]

    for at, n in geo.chunks:
        patches = jnp.concatenate(
            [x0[:, MARGIN + at + geo.offset(*s) : MARGIN + at + geo.offset(*s) + n] for s in SHIFTS], axis=0
        ).astype(BF16)
        y, slope = silu_parts(mm(w1_f, patches))
        act1[:, MARGIN + at : MARGIN + at + n] = (y * mask_s[:1, at : at + n]).astype(BF16)
        sl1[:, at : at + n] = slope

    def fine_patches(ref, at, n):
        blocks = []
        for y, x in PATCH:
            p = 2 * (y % 2) + x % 2
            start = MARGIN + at + geo.offset(y // 2, x // 2)
            blocks.append(ref[p * f1 : (p + 1) * f1, start : start + n])
        return jnp.concatenate(blocks, axis=0)

    def coarse_patches(ref, at, n, sign):
        blocks = []
        for s in SHIFTS:
            start = MARGIN + at + sign * geo.offset(*s)
            blocks.append(ref[:, start : start + n])
        return jnp.concatenate(blocks, axis=0)

    for at, n in geo.chunks:
        y, slope = silu_parts(mm(w2_f, fine_patches(act1, at, n)))
        sl2[:, at : at + n] = slope
        y, slope = silu_parts(mm(ws_f, y.astype(BF16)))
        act_s[:, MARGIN + at : MARGIN + at + n] = (y * mask_s[:1, at : at + n]).astype(BF16)
        sls[:, at : at + n] = slope
    for at, n in geo.chunks:
        y, slope = silu_parts(mm(w3_f, coarse_patches(act_s, at, n, 1)))
        logits = mm(head_row, y.astype(BF16))
        log_s[:, at : at + n] = logits
        out = (0.5 * jnp.tanh(0.5 * logits) + 0.5 - targ_s[:, at : at + n]) * mask_s[:, at : at + n]
        dl3[:, MARGIN + at : MARGIN + at + n] = (head_col * out[:1] * slope).astype(BF16)
    for at, n in geo.chunks:
        back = mm(w3_b, coarse_patches(dl3, at, n, -1))
        back = mm(ws_b, (back * sls[:, at : at + n]).astype(BF16))
        dl2[:, MARGIN + at : MARGIN + at + n] = (
            back * sl2[:, at : at + n] * mask_s[:1, at : at + n]
        ).astype(BF16)
    for at, n in geo.chunks:
        back = mm(w2_b, fine_patches(dl2, at, n))
        delta = (back * sl1[:, at : at + n] * mask_s[:1, at : at + n]).astype(BF16)
        zs[:, MARGIN + at : MARGIN + at + n] = mm(w1_b, delta)
    for at, n in geo.chunks:
        total = None
        for s, shift in enumerate(SHIFTS):
            start = MARGIN + at - geo.offset(*shift)
            term = zs[8 * s : 8 * s + 8, start : start + n]
            total = term if total is None else total + term
        grad_s[:, at : at + n] = total
    for r in range(rows):
        at = (r + HALO) * pitch + HALO
        logit_o[r : r + 1, :] = log_s[:1, at : at + cols]
    spread = None
    lane = lax.broadcasted_iota(jnp.int32, (cols, 2 * cols), 1)
    sub = lax.broadcasted_iota(jnp.int32, (cols, 2 * cols), 0)
    for b in range(2):
        for r in range(rows):
            at = (r + HALO) * pitch + HALO
            for a in range(2):
                un[2 * r + a : 2 * r + a + 1, :cols] = grad_s[2 * a + b : 2 * a + b + 1, at : at + cols]
        g_h, g_l = split(un[: 2 * rows, :cols])
        place = jnp.where(lane == 2 * sub + b, 1.0, 0.0).astype(BF16)
        term = mm(g_h, place) + mm(g_l, place)
        spread = term if spread is None else spread + term
    grad_o[...] = spread


def unet_scratch(geo, f1, f2):
    return [
        pltpu.VMEM((8, geo.width), F32),
        pltpu.VMEM((8, geo.padded), F32),
        pltpu.VMEM((8, geo.padded), F32),
        pltpu.VMEM((4 * f1, geo.width), BF16),
        pltpu.VMEM((4 * f1, geo.padded), F32),
        pltpu.VMEM((4 * f1, geo.padded), F32),
        pltpu.VMEM((f2, geo.width), BF16),
        pltpu.VMEM((f2, geo.padded), F32),
        pltpu.VMEM((f2, geo.width), BF16),
        pltpu.VMEM((4 * f1, geo.width), BF16),
        pltpu.VMEM((72, geo.width), F32),
        pltpu.VMEM((8, geo.padded), F32),
        pltpu.VMEM((8, geo.padded), F32),
        pltpu.VMEM((2 * geo.high, -(-geo.pitch // 128) * 128), F32),
    ]


def out_shapes(geo):
    return (
        jax.ShapeDtypeStruct((2 * geo.rows, 2 * geo.cols), BF16),
        jax.ShapeDtypeStruct((geo.rows, geo.cols), F32),
        jax.ShapeDtypeStruct((2 * geo.rows, 2 * geo.cols), F32),
    )


def step_kernel(geo, samples, total_rows, freqs, pb, freq, pick, w1, w2, ws, w3, wh, *rest):
    me_ch, me_t = lax.axis_index("ch"), lax.axis_index("tm") * lax.axis_size("sub") + lax.axis_index("sub")
    unet(
        geo, samples, total_rows, pb[...], freq[...], freqs, pick[...], me_ch, me_t,
        (w1, w2, ws, w3, wh), rest[:3], rest[3:],
    )


def wave_tables(total, channels_out=None):
    index = jnp.arange(total, dtype=jnp.int32)
    angle = (index[:, None] * index[None, :] % total).astype(F32) * (2.0 * math.pi / total)
    return jnp.cos(angle), jnp.sin(angle)


def spectral_wide(record, freq_bins, wave_limit, geo, samples, total_chans):
    precise = lax.Precision.HIGHEST
    local_chans, local_times = record.shape
    chan_groups = lax.axis_size("ch")
    time_groups = lax.axis_size(("tm", "sub"))
    freq_count = freq_bins.shape[0]
    bins_local = freq_count // (chan_groups * time_groups)
    time_index = lax.axis_index(("tm", "sub")) * local_times + jnp.arange(local_times, dtype=jnp.int32)
    angle = (freq_bins[:, None] * time_index[None, :] % samples).astype(F32) * (2.0 * math.pi / samples)
    signal = record.astype(F32)
    real_part = jnp.einsum("ft,ct->fc", jnp.cos(angle), signal, precision=precise)
    imag_part = -jnp.einsum("ft,ct->fc", jnp.sin(angle), signal, precision=precise)
    summed = lax.psum_scatter(
        jnp.concatenate([real_part, imag_part], axis=1), ("tm", "sub"), scatter_dimension=0, tiled=True
    )
    gathered = lax.all_to_all(summed.astype(BF16), "ch", split_axis=0, concat_axis=1, tiled=True)
    block = lax.axis_index(("tm", "sub")) * chan_groups + lax.axis_index("ch")
    arranged = gathered.reshape(bins_local, chan_groups, 2, local_chans).transpose(2, 0, 1, 3)
    arranged = arranged.reshape(2, bins_local, total_chans).astype(F32)
    limits = lax.dynamic_slice_in_dim(wave_limit, block * bins_local, bins_local)
    cosine, sine = wave_tables(total_chans)
    dot = functools.partial(jnp.dot, precision=precise)
    re = dot(arranged[0], cosine) + dot(arranged[1], sine)
    im = dot(arranged[1], cosine) - dot(arranged[0], sine)
    index = jnp.arange(total_chans, dtype=jnp.int32)
    passing = jnp.minimum(index, total_chans - index)[None] <= limits[:, None]
    re, im = jnp.where(passing, re, 0.0), jnp.where(passing, im, 0.0)
    out = jnp.stack([dot(re, cosine) - dot(im, sine), dot(im, cosine) + dot(re, sine)]) / total_chans
    out = jnp.pad(out.astype(BF16), ((0, 0), (0, 0), (2 * HALO, 2 * HALO)))
    wide = local_chans + 4 * HALO
    outgoing = jnp.stack([out[:, :, g * local_chans : g * local_chans + wide] for g in range(chan_groups)])
    outgoing = outgoing.transpose(2, 0, 1, 3).reshape(bins_local, chan_groups * 2 * wide)
    returned = lax.all_to_all(outgoing, "ch", split_axis=1, concat_axis=0, tiled=True)
    values = lax.all_gather(returned, ("tm", "sub"), axis=0, tiled=True)
    return values.reshape(freq_count, 2, wide).transpose(2, 1, 0).reshape(wide, 2 * freq_count)


def local(record, freq_bins, wave_limit, pick_index, w1, w2, ws, w3, wh):
    local_chans, local_times = record.shape
    chan_groups = lax.axis_size("ch")
    samples = local_times * lax.axis_size(("tm", "sub"))
    total_chans = local_chans * chan_groups
    freqs = freq_bins.shape[0]
    geo = Geometry(local_chans // 2, local_times // 2)
    pb = spectral_wide(record, freq_bins, wave_limit, geo, samples, total_chans)
    freq_row = jnp.concatenate([freq_bins, freq_bins])[None]
    picks = jnp.pad(lax.all_gather(pick_index, "ch", axis=0, tiled=True), (HALO, HALO))
    picks = lax.dynamic_slice_in_dim(picks, lax.axis_index("ch") * geo.rows, geo.high)
    vmem = pl.BlockSpec(memory_space=pltpu.VMEM)
    return pl.pallas_call(
        functools.partial(step_kernel, geo, samples, total_chans // 2, freqs),
        out_shape=out_shapes(geo),
        in_specs=[vmem] * 8,
        out_specs=(vmem,) * 3,
        scratch_shapes=unet_scratch(geo, w2.shape[1], w3.shape[1]),
        compiler_params=pltpu.CompilerParams(vmem_limit_bytes=48 * 2**20),
    )(pb, freq_row, picks.astype(F32)[:, None], w1, w2, ws, w3, wh[None])


def solution(mesh):
    return jax.shard_map(
        local,
        mesh=mesh,
        in_specs=(
            P(("grp", "ch"), ("tm", "sub")),
            P("grp"),
            P("grp"),
            P(("grp", "ch")),
            P(),
            P(),
            P(),
            P(),
            P(),
        ),
        out_specs=(P(("grp", "ch"), ("tm", "sub")),) * 3,
        check_vma=False,
    )
```

```python
import functools
import math

import jax
import jax.numpy as jnp
from jax import lax
from jax.experimental import pallas as pl
from jax.experimental.pallas import tpu as pltpu
from jax.sharding import PartitionSpec as P

SIGMA = 64
HALO = 4
MARGIN = 256
F32 = jnp.float32
BF16 = jnp.bfloat16
SHIFTS = [(sy, sx) for sy in (-1, 0, 1) for sx in (-1, 0, 1)]
PATCH = [(y, x) for y in (-1, 0, 1, 2) for x in (-1, 0, 1, 2)]


def mm(lhs, rhs):
    return jnp.dot(lhs, rhs, preferred_element_type=F32)


def mm_nt(lhs, rhs):
    return lax.dot_general(lhs, rhs, (((1,), (1,)), ((), ())), preferred_element_type=F32)


def split(value):
    high = value.astype(BF16)
    return high, (value - high.astype(F32)).astype(BF16)


def cosine_turns(count, samples):
    folded = jnp.abs(count - samples // 2).astype(F32)
    z = folded * (2.0 * math.pi / samples) - (math.pi / 2)
    z2 = z * z
    poly = jnp.full_like(z2, -1.0 / 39916800)
    for term in (362880, -5040, 120, -6, 1):
        poly = poly * z2 + 1.0 / term
    return z * poly


def table(freq_row, freqs, first_time, step, length, samples):
    time = first_time + step * lax.broadcasted_iota(jnp.int32, (length, 2 * freqs), 0)
    lane = lax.broadcasted_iota(jnp.int32, (length, 2 * freqs), 1)
    quarter = jnp.where(lane >= freqs, samples // 4, 0)
    return cosine_turns((freq_row * time + quarter) & (samples - 1), samples)


def silu_parts(v):
    s = 0.5 * jnp.tanh(0.5 * v) + 0.5
    y = v * s
    return y, s + y * (1.0 - s)


class Geometry:
    def __init__(self, rows, cols):
        self.rows, self.cols = rows, cols
        self.high = rows + 2 * HALO
        self.pitch = cols + 2 * HALO
        self.size = self.high * self.pitch
        self.padded = -(-self.size // 256) * 256
        self.width = self.padded + 2 * MARGIN
        count = 2
        tiles = self.padded // 128
        self.chunks = []
        at = 0
        for i in range(count):
            end = tiles * (i + 1) // count
            self.chunks.append((at * 128, (end - at) * 128))
            at = end

    def offset(self, sy, sx):
        return sy * self.pitch + sx


def unet(geo, samples, total_rows, pb, freq_row, freqs, pick_col, me_ch, me_t, refs, outs, scr):
    w1_ref, w2_ref, ws_ref, w3_ref, wh_ref = refs
    filt_o, logit_o, grad_o = outs
    x0, mask_s, targ_s, act1, sl1, sl2, act_s, sls, dl3, dl2, zs, log_s, grad_s, un = scr
    rows, cols, pitch = geo.rows, geo.cols, geo.pitch
    total_cols = samples // 2
    scale = 2.0 / samples
    f1 = w2_ref.shape[1]
    for ref in (x0, act1, act_s, dl3, dl2, zs):
        n = ref.shape[0]
        ref[:, :MARGIN] = jnp.zeros((n, MARGIN), ref.dtype)
        ref[:, MARGIN + geo.padded :] = jnp.zeros((n, MARGIN), ref.dtype)
    place = lax.broadcasted_iota(jnp.int32, (8, geo.padded), 1).astype(F32)[:1]
    row = jnp.floor((place + 0.5) * (1.0 / pitch))
    col = place - row * pitch
    grow = row + (me_ch * rows - HALO).astype(F32)
    gcol = col + (me_t * cols - HALO).astype(F32)
    inside = (grow >= 0) & (grow < total_rows) & (gcol >= 0) & (gcol < total_cols) & (row < geo.high)
    mask = jnp.where(inside, 1.0, 0.0)
    mask_s[...] = jnp.broadcast_to(mask, mask_s.shape)
    rid = lax.broadcasted_iota(jnp.int32, (geo.high, geo.padded), 0).astype(F32)
    pick = jnp.sum(jnp.where(rid == row, pick_col, 0.0), axis=0, keepdims=True)
    offs = (2.0 * gcol - pick) * (1.0 / SIGMA)
    targ_s[...] = jnp.broadcast_to(jnp.exp(-0.5 * offs * offs), targ_s.shape)
    w2 = [w2_ref[k].astype(F32) for k in range(9)]
    zero = jnp.zeros_like(w2[0])

    def tap(y, x, a, b, sign):
        ky, kx = sign * (y - a) + 1, sign * (x - b) + 1
        return w2[3 * ky + kx] if 0 <= ky < 3 and 0 <= kx < 3 else zero

    phases = [(a, b) for a in (0, 1) for b in (0, 1)]
    w2_f = jnp.concatenate(
        [jnp.concatenate([tap(y, x, a, b, 1) for y, x in PATCH], axis=1) for a, b in phases], axis=0
    ).astype(BF16)
    w2_b = jnp.concatenate(
        [jnp.concatenate([tap(y, x, a, b, -1) for a, b in phases], axis=1) for y, x in PATCH], axis=0
    ).T.astype(BF16)
    ws_f32 = jnp.concatenate([ws_ref[k].astype(F32) for k in range(4)], axis=1)
    ws_f, ws_b = ws_f32.astype(BF16), ws_f32.T.astype(BF16)
    w3 = [w3_ref[k].astype(F32) for k in range(9)]
    w3_f = jnp.concatenate(w3, axis=1).astype(BF16)
    w3_b = jnp.concatenate(w3, axis=0).T.astype(BF16)
    head = jnp.broadcast_to(wh_ref[...].astype(F32), (8, wh_ref.shape[1]))
    head_col = head.T[:, :1]
    head_row = head.astype(BF16)
    srow = lax.broadcasted_iota(jnp.int32, (72, 9), 0)
    tapi = lax.broadcasted_iota(jnp.int32, (72, 9), 1)
    w1 = w1_ref[...]
    parts = []
    for a, b in phases:
        sel = jnp.zeros((72, 9), F32)
        for s, (sy, sx) in enumerate(SHIFTS):
            for p, (py, px) in enumerate(phases):
                ky, kx = 2 * sy + py - a + 1, 2 * sx + px - b + 1
                if 0 <= ky < 3 and 0 <= kx < 3:
                    sel = jnp.where((srow == 8 * s + p) & (tapi == 3 * ky + kx), 1.0, sel)
        parts.append(mm(sel.astype(BF16), w1))
    w1_b32 = jnp.concatenate(parts, axis=1)
    w1_f, w1_b = w1_b32.T.astype(BF16), w1_b32.astype(BF16)

    nat_h, nat_l = split(table(freq_row, freqs, me_t * 2 * cols, 1, 2 * cols, samples))
    nat = (mm_nt(pb, nat_h) + mm_nt(pb, nat_l)) * scale
    filt_o[...] = nat[2 * HALO : 2 * HALO + 2 * rows].astype(BF16)
    x0[...] = jnp.zeros_like(x0)
    for b in range(2):
        t_h, t_l = split(
            table(freq_row, freqs, me_t * 2 * cols - 2 * HALO + b, 2, geo.pitch, samples)
        )
        un[:, :pitch] = (mm_nt(pb, t_h) + mm_nt(pb, t_l)) * scale
        for r in range(geo.high):
            at = MARGIN + r * pitch
            for a in range(2):
                x0[2 * a + b : 2 * a + b + 1, at : at + pitch] = un[2 * r + a : 2 * r + a + 1, :pitch]
    x0[:, MARGIN : MARGIN + geo.padded] = x0[:, MARGIN : MARGIN + geo.padded] * mask_s[...]

    for at, n in geo.chunks:
        patches = jnp.concatenate(
            [x0[:, MARGIN + at + geo.offset(*s) : MARGIN + at + geo.offset(*s) + n] for s in SHIFTS], axis=0
        ).astype(BF16)
        y, slope = silu_parts(mm(w1_f, patches))
        act1[:, MARGIN + at : MARGIN + at + n] = (y * mask_s[:1, at : at + n]).astype(BF16)
        sl1[:, at : at + n] = slope

    def fine_patches(ref, at, n):
        blocks = []
        for y, x in PATCH:
            p = 2 * (y % 2) + x % 2
            start = MARGIN + at + geo.offset(y // 2, x // 2)
            blocks.append(ref[p * f1 : (p + 1) * f1, start : start + n])
        return jnp.concatenate(blocks, axis=0)

    def coarse_patches(ref, at, n, sign):
        blocks = []
        for s in SHIFTS:
            start = MARGIN + at + sign * geo.offset(*s)
            blocks.append(ref[:, start : start + n])
        return jnp.concatenate(blocks, axis=0)

    for at, n in geo.chunks:
        y, slope = silu_parts(mm(w2_f, fine_patches(act1, at, n)))
        sl2[:, at : at + n] = slope
        y, slope = silu_parts(mm(ws_f, y.astype(BF16)))
        act_s[:, MARGIN + at : MARGIN + at + n] = (y * mask_s[:1, at : at + n]).astype(BF16)
        sls[:, at : at + n] = slope
    for at, n in geo.chunks:
        y, slope = silu_parts(mm(w3_f, coarse_patches(act_s, at, n, 1)))
        logits = mm(head_row, y.astype(BF16))
        log_s[:, at : at + n] = logits
        out = (0.5 * jnp.tanh(0.5 * logits) + 0.5 - targ_s[:, at : at + n]) * mask_s[:, at : at + n]
        dl3[:, MARGIN + at : MARGIN + at + n] = (head_col * out[:1] * slope).astype(BF16)
    for at, n in geo.chunks:
        back = mm(w3_b, coarse_patches(dl3, at, n, -1))
        back = mm(ws_b, (back * sls[:, at : at + n]).astype(BF16))
        dl2[:, MARGIN + at : MARGIN + at + n] = (
            back * sl2[:, at : at + n] * mask_s[:1, at : at + n]
        ).astype(BF16)
    for at, n in geo.chunks:
        back = mm(w2_b, fine_patches(dl2, at, n))
        delta = (back * sl1[:, at : at + n] * mask_s[:1, at : at + n]).astype(BF16)
        zs[:, MARGIN + at : MARGIN + at + n] = mm(w1_b, delta)
    for at, n in geo.chunks:
        total = None
        for s, shift in enumerate(SHIFTS):
            start = MARGIN + at - geo.offset(*shift)
            term = zs[8 * s : 8 * s + 8, start : start + n]
            total = term if total is None else total + term
        grad_s[:, at : at + n] = total
    for r in range(rows):
        at = (r + HALO) * pitch + HALO
        logit_o[r : r + 1, :] = log_s[:1, at : at + cols]
    spread = None
    lane = lax.broadcasted_iota(jnp.int32, (cols, 2 * cols), 1)
    sub = lax.broadcasted_iota(jnp.int32, (cols, 2 * cols), 0)
    for b in range(2):
        for r in range(rows):
            at = (r + HALO) * pitch + HALO
            for a in range(2):
                un[2 * r + a : 2 * r + a + 1, :cols] = grad_s[2 * a + b : 2 * a + b + 1, at : at + cols]
        g_h, g_l = split(un[: 2 * rows, :cols])
        place = jnp.where(lane == 2 * sub + b, 1.0, 0.0).astype(BF16)
        term = mm(g_h, place) + mm(g_l, place)
        spread = term if spread is None else spread + term
    grad_o[...] = spread


def unet_scratch(geo, f1, f2):
    return [
        pltpu.VMEM((8, geo.width), F32),
        pltpu.VMEM((8, geo.padded), F32),
        pltpu.VMEM((8, geo.padded), F32),
        pltpu.VMEM((4 * f1, geo.width), BF16),
        pltpu.VMEM((4 * f1, geo.padded), F32),
        pltpu.VMEM((4 * f1, geo.padded), F32),
        pltpu.VMEM((f2, geo.width), BF16),
        pltpu.VMEM((f2, geo.padded), F32),
        pltpu.VMEM((f2, geo.width), BF16),
        pltpu.VMEM((4 * f1, geo.width), BF16),
        pltpu.VMEM((72, geo.width), F32),
        pltpu.VMEM((8, geo.padded), F32),
        pltpu.VMEM((8, geo.padded), F32),
        pltpu.VMEM((2 * geo.high, -(-geo.pitch // 128) * 128), F32),
    ]


def out_shapes(geo):
    return (
        jax.ShapeDtypeStruct((2 * geo.rows, 2 * geo.cols), BF16),
        jax.ShapeDtypeStruct((geo.rows, geo.cols), F32),
        jax.ShapeDtypeStruct((2 * geo.rows, 2 * geo.cols), F32),
    )


def step_kernel(geo, samples, total_rows, freqs, pb, freq, pick, w1, w2, ws, w3, wh, *rest):
    me_ch, me_t = lax.axis_index("ch"), lax.axis_index("tm") * lax.axis_size("sub") + lax.axis_index("sub")
    unet(
        geo, samples, total_rows, pb[...], freq[...], freqs, pick[...], me_ch, me_t,
        (w1, w2, ws, w3, wh), rest[:3], rest[3:],
    )


def exchange_kernel(samples, record, freq, pick, out, mine, landed, gath, sems_t, sems_c):
    grp, ch, tm, sub = (lax.axis_index(name) for name in ("grp", "ch", "tm", "sub"))
    groups = lax.axis_size("ch")
    time_partners = [(tm, 1 - sub), (1 - tm, sub), (1 - tm, 1 - sub)]
    targets = [(grp, ch, t, s) for t, s in time_partners]
    targets += [(grp, lax.rem(ch + d, groups), tm, sub) for d in range(1, groups)]
    barrier = pltpu.get_barrier_semaphore()
    for target in targets:
        pl.semaphore_signal(barrier, inc=1, device_id=target, device_id_type=pl.DeviceIdType.MESH)
    chans, times = record.shape
    freqs = freq.shape[1]
    half = chans // 2
    freq_row = jnp.concatenate([freq[...], freq[...]], axis=1)
    high, low = split(table(freq_row, freqs, (tm * 2 + sub) * times, 1, times, samples))
    part = mm(record[...], high) + mm(record[...], low)
    mine[...] = jnp.concatenate([part[:half], part[half:]], axis=1)
    pl.semaphore_wait(barrier, len(targets))
    copies = []
    for d in range(3):
        copies.append(
            pltpu.make_async_remote_copy(
                src_ref=mine,
                dst_ref=landed.at[d],
                send_sem=sems_t.at[0, d],
                recv_sem=sems_t.at[1, d],
                device_id=targets[d],
                device_id_type=pl.DeviceIdType.MESH,
            )
        )
        copies[-1].start()
    picks = jnp.broadcast_to(pick[...], (8, pick.shape[1])).astype(F32).T[:, :1]
    coarse = jnp.floor(picks * 0.125)
    side = jnp.concatenate([coarse, picks - 8.0 * coarse], axis=1)
    side = jnp.concatenate([side, jnp.zeros((half, 2 * freqs - 2), F32)], axis=1)
    side = jnp.concatenate([side, jnp.zeros_like(side)], axis=0)
    for copy in copies:
        copy.wait()
    total = (mine[...] + landed[0]) + (landed[1] + landed[2])
    spectrum = jnp.concatenate([total[:, : 2 * freqs], total[:, 2 * freqs :]], axis=0)
    gath[ch] = jnp.concatenate([spectrum, side], axis=1).astype(BF16)
    copies = []
    for d in range(1, groups):
        copies.append(
            pltpu.make_async_remote_copy(
                src_ref=gath.at[ch],
                dst_ref=gath.at[ch],
                send_sem=sems_c.at[0, d - 1],
                recv_sem=sems_c.at[1, d - 1],
                device_id=targets[2 + d],
                device_id_type=pl.DeviceIdType.MESH,
            )
        )
        copies[-1].start()
    for copy in copies:
        copy.wait()
    out[...] = gath[...]


def exchange(record, freq_bins, pick_index, samples):
    groups = lax.axis_size("ch")
    chans = record.shape[0]
    lanes = 4 * freq_bins.shape[0]
    vmem = pl.BlockSpec(memory_space=pltpu.VMEM)
    return pl.pallas_call(
        functools.partial(exchange_kernel, samples),
        out_shape=jax.ShapeDtypeStruct((groups, chans, lanes), BF16),
        in_specs=[vmem] * 3,
        out_specs=vmem,
        scratch_shapes=[
            pltpu.VMEM((chans // 2, lanes), F32),
            pltpu.VMEM((3, chans // 2, lanes), F32),
            pltpu.VMEM((groups, chans, lanes), BF16),
            pltpu.SemaphoreType.DMA((2, 3)),
            pltpu.SemaphoreType.DMA((2, groups - 1)),
        ],
        compiler_params=pltpu.CompilerParams(collective_id=0, has_side_effects=True),
    )(record, freq_bins[None], pick_index[None])


def dft_table(first_row, rows, total):
    at = first_row + lax.broadcasted_iota(jnp.int32, (rows, 2 * total), 0)
    lane = lax.broadcasted_iota(jnp.int32, (rows, 2 * total), 1)
    quarter = jnp.where(lane >= total, 3 * total // 4, 0)
    return split(cosine_turns((at * (lane & (total - 1)) + quarter) & (total - 1), total))


def small_kernel(geo, samples, freqs, gath, freq, limit, w1, w2, ws, w3, wh, *rest):
    me_ch, me_t = lax.axis_index("ch"), lax.axis_index("tm") * lax.axis_size("sub") + lax.axis_index("sub")
    groups, chans, _ = gath.shape
    total = groups * chans
    both = 2 * freqs
    spec = jnp.concatenate([gath[g].astype(F32) for g in range(groups)], axis=0)
    re, im = spec[:, :freqs], spec[:, freqs:both]
    stack = jnp.concatenate(
        [jnp.concatenate([re, im], axis=1), jnp.concatenate([im, -re], axis=1)], axis=0
    ).astype(BF16)
    high, low = dft_table(0, total, total)
    wave = mm(high, stack) + mm(low, stack)
    index = lax.broadcasted_iota(jnp.int32, (total, both), 0)
    limits = jnp.concatenate([limit[...], limit[...]], axis=1)
    wave = jnp.where(jnp.minimum(index, total - index) <= limits, wave, 0.0)
    re, im = wave[:, :freqs], wave[:, freqs:]
    stack_h, stack_l = split(jnp.concatenate([wave, jnp.concatenate([-im, re], axis=1)], axis=0))
    high, low = dft_table(me_ch * chans - 2 * HALO + total, chans + 4 * HALO, total)
    pb = (mm(high, stack_h) + mm(low, stack_h) + mm(high, stack_l)) * (1.0 / total)
    around = [jnp.maximum(me_ch - 1, 0), me_ch, jnp.minimum(me_ch + 1, groups - 1)]
    rows = geo.rows
    picks = []
    for g, (first, last) in zip(around, ((rows - HALO, rows), (0, rows), (0, HALO))):
        side = gath[g].astype(F32)[first:last]
        picks.append(side[:, both : both + 1] * 8.0 + side[:, both + 1 : both + 2])
    pick_col = jnp.concatenate(picks, axis=0)
    freq_row = jnp.concatenate([freq[...], freq[...]], axis=1)
    unet(
        geo, samples, total // 2, pb.astype(BF16), freq_row, freqs, pick_col, me_ch, me_t,
        (w1, w2, ws, w3, wh), rest[:3], rest[3:],
    )


def wave_tables(total):
    index = jnp.arange(total, dtype=jnp.int32)
    angle = (index[:, None] * index[None, :] % total).astype(F32) * (2.0 * math.pi / total)
    return jnp.cos(angle), jnp.sin(angle)


def spectral_wide(record, freq_bins, wave_limit, geo, samples, total_chans):
    precise = lax.Precision.HIGHEST
    local_chans, local_times = record.shape
    chan_groups = lax.axis_size("ch")
    time_groups = lax.axis_size(("tm", "sub"))
    freq_count = freq_bins.shape[0]
    bins_local = freq_count // (chan_groups * time_groups)
    time_index = lax.axis_index(("tm", "sub")) * local_times + jnp.arange(local_times, dtype=jnp.int32)
    angle = (freq_bins[:, None] * time_index[None, :] % samples).astype(F32) * (2.0 * math.pi / samples)
    signal = record.astype(F32)
    real_part = jnp.einsum("ft,ct->fc", jnp.cos(angle), signal, precision=precise)
    imag_part = -jnp.einsum("ft,ct->fc", jnp.sin(angle), signal, precision=precise)
    summed = lax.psum_scatter(
        jnp.concatenate([real_part, imag_part], axis=1), ("tm", "sub"), scatter_dimension=0, tiled=True
    )
    gathered = lax.all_to_all(summed.astype(BF16), "ch", split_axis=0, concat_axis=1, tiled=True)
    block = lax.axis_index(("tm", "sub")) * chan_groups + lax.axis_index("ch")
    arranged = gathered.reshape(bins_local, chan_groups, 2, local_chans).transpose(2, 0, 1, 3)
    arranged = arranged.reshape(2, bins_local, total_chans).astype(F32)
    limits = lax.dynamic_slice_in_dim(wave_limit, block * bins_local, bins_local)
    cosine, sine = wave_tables(total_chans)
    dot = functools.partial(jnp.dot, precision=precise)
    re = dot(arranged[0], cosine) + dot(arranged[1], sine)
    im = dot(arranged[1], cosine) - dot(arranged[0], sine)
    index = jnp.arange(total_chans, dtype=jnp.int32)
    passing = jnp.minimum(index, total_chans - index)[None] <= limits[:, None]
    re, im = jnp.where(passing, re, 0.0), jnp.where(passing, im, 0.0)
    out = jnp.stack([dot(re, cosine) - dot(im, sine), dot(im, cosine) + dot(re, sine)]) / total_chans
    out = jnp.pad(out.astype(BF16), ((0, 0), (0, 0), (2 * HALO, 2 * HALO)))
    wide = local_chans + 4 * HALO
    outgoing = jnp.stack([out[:, :, g * local_chans : g * local_chans + wide] for g in range(chan_groups)])
    outgoing = outgoing.transpose(2, 0, 1, 3).reshape(bins_local, chan_groups * 2 * wide)
    returned = lax.all_to_all(outgoing, "ch", split_axis=1, concat_axis=0, tiled=True)
    values = lax.all_gather(returned, ("tm", "sub"), axis=0, tiled=True)
    return values.reshape(freq_count, 2, wide).transpose(2, 1, 0).reshape(wide, 2 * freq_count)


def local(record, freq_bins, wave_limit, pick_index, w1, w2, ws, w3, wh):
    local_chans, local_times = record.shape
    chan_groups = lax.axis_size("ch")
    samples = local_times * lax.axis_size(("tm", "sub"))
    total_chans = local_chans * chan_groups
    freqs = freq_bins.shape[0]
    geo = Geometry(local_chans // 2, local_times // 2)
    vmem = pl.BlockSpec(memory_space=pltpu.VMEM)
    call = dict(
        out_shape=out_shapes(geo),
        in_specs=[vmem] * 8,
        out_specs=(vmem,) * 3,
        scratch_shapes=unet_scratch(geo, w2.shape[1], w3.shape[1]),
        compiler_params=pltpu.CompilerParams(vmem_limit_bytes=48 * 2**20),
    )
    if lax.axis_size("tm") == 2 and lax.axis_size("sub") == 2 and freqs == 32 and total_chans <= 256:
        gath = exchange(record, freq_bins, pick_index, samples)
        return pl.pallas_call(functools.partial(small_kernel, geo, samples, freqs), **call)(
            gath, freq_bins[None], wave_limit[None], w1, w2, ws, w3, wh[None]
        )
    pb = spectral_wide(record, freq_bins, wave_limit, geo, samples, total_chans)
    freq_row = jnp.concatenate([freq_bins, freq_bins])[None]
    picks = jnp.pad(lax.all_gather(pick_index, "ch", axis=0, tiled=True), (HALO, HALO))
    picks = lax.dynamic_slice_in_dim(picks, lax.axis_index("ch") * geo.rows, geo.high)
    return pl.pallas_call(
        functools.partial(step_kernel, geo, samples, total_chans // 2, freqs), **call
    )(pb, freq_row, picks.astype(F32)[:, None], w1, w2, ws, w3, wh[None])


def solution(mesh):
    return jax.shard_map(
        local,
        mesh=mesh,
        in_specs=(
            P(("grp", "ch"), ("tm", "sub")),
            P("grp"),
            P("grp"),
            P(("grp", "ch")),
            P(),
            P(),
            P(),
            P(),
            P(),
        ),
        out_specs=(P(("grp", "ch"), ("tm", "sub")),) * 3,
        check_vma=False,
    )
```

```python
import functools
import math

import jax
import jax.numpy as jnp
from jax import lax
from jax.experimental import pallas as pl
from jax.experimental.pallas import tpu as pltpu
from jax.sharding import PartitionSpec as P

SIGMA = 64
HALO = 4
MARGIN = 256
F32 = jnp.float32
BF16 = jnp.bfloat16
PHASES = [(a, b) for a in (0, 1) for b in (0, 1)]
SHIFTS = [(sy, sx) for sy in (-1, 0, 1) for sx in (-1, 0, 1)]
PATCH = [(y, x) for y in (-1, 0, 1, 2) for x in (-1, 0, 1, 2)]


def mm(lhs, rhs):
    return jnp.dot(lhs, rhs, preferred_element_type=F32)


def mm_nt(lhs, rhs):
    return lax.dot_general(lhs, rhs, (((1,), (1,)), ((), ())), preferred_element_type=F32)


def split(value):
    high = value.astype(BF16)
    return high, (value - high.astype(F32)).astype(BF16)


def cosine_turns(count, samples):
    folded = jnp.abs(count - samples // 2).astype(F32)
    z = folded * (2.0 * math.pi / samples) - (math.pi / 2)
    z2 = z * z
    poly = jnp.full_like(z2, -1.0 / 39916800)
    for term in (362880, -5040, 120, -6, 1):
        poly = poly * z2 + 1.0 / term
    return z * poly


def table(freq_row, freqs, first_time, step, length, samples):
    time = first_time + step * lax.broadcasted_iota(jnp.int32, (length, 2 * freqs), 0)
    lane = lax.broadcasted_iota(jnp.int32, (length, 2 * freqs), 1)
    quarter = jnp.where(lane >= freqs, samples // 4, 0)
    return cosine_turns((freq_row * time + quarter) & (samples - 1), samples)


def silu_parts(v):
    s = 0.5 * jnp.tanh(0.5 * v) + 0.5
    y = v * s
    return y, s + y * (1.0 - s)


class Geometry:
    def __init__(self, rows, cols):
        self.rows, self.cols = rows, cols
        self.high = rows + 2 * HALO
        self.pitch = cols + 2 * HALO
        self.size = self.high * self.pitch
        self.padded = -(-self.size // 256) * 256
        self.width = self.padded + 2 * MARGIN

    def chunks(self, margin, count=2):
        first = margin * self.pitch // 128
        last = -(-(self.high - margin) * self.pitch // 128)
        last += (last - first) % 2
        cuts = [first + (last - first) * i // count for i in range(count + 1)]
        return [(lo * 128, (hi - lo) * 128) for lo, hi in zip(cuts, cuts[1:])]

    def offset(self, sy, sx):
        return sy * self.pitch + sx


def conv_weights(w2_in, ws_in, w3_in):
    w2 = [w2_in[k].astype(F32) for k in range(9)]
    zero = jnp.zeros_like(w2[0])

    def tap(y, x, a, b, sign):
        ky, kx = sign * (y - a) + 1, sign * (x - b) + 1
        return w2[3 * ky + kx] if 0 <= ky < 3 and 0 <= kx < 3 else zero

    w2_f = jnp.concatenate(
        [jnp.concatenate([tap(y, x, a, b, 1) for y, x in PATCH], axis=1) for a, b in PHASES], axis=0
    ).astype(BF16)
    w2_b = jnp.concatenate(
        [jnp.concatenate([tap(y, x, a, b, -1) for a, b in PHASES], axis=1) for y, x in PATCH], axis=0
    ).T.astype(BF16)
    ws_f32 = jnp.concatenate([ws_in[k].astype(F32) for k in range(4)], axis=0)
    ws_f, ws_b = ws_f32.T.astype(BF16), ws_f32.astype(BF16)
    w3 = [w3_in[k].astype(F32) for k in range(9)]
    w3_f = jnp.concatenate(w3, axis=1).astype(BF16)
    w3_b = jnp.concatenate(w3, axis=0).T.astype(BF16)
    return w2_f, w2_b, ws_f, ws_b, w3_f, w3_b


def unet_tables(freq_row, freqs, me_t, geo, samples):
    first = me_t * 2 * geo.cols
    found = split(table(freq_row, freqs, first, 1, 2 * geo.cols, samples))
    for b in range(2):
        found += split(table(freq_row, freqs, first - 2 * HALO + b, 2, geo.pitch, samples))
    return found


def unet(geo, samples, total_rows, pb, tables, pick_col, me_ch, me_t, w1_ref, wh_ref, convs, outs, scr):
    filt_o, logit_o, grad_o = outs
    x0, mask_s, targ_s, act1, sl1, sl2, act_s, sls, dl3, dl2, zs, log_s, grad_s, un = scr
    rows, cols, pitch = geo.rows, geo.cols, geo.pitch
    total_cols = samples // 2
    scale = 2.0 / samples
    f1 = w1_ref.shape[1]
    for ref, margin in ((x0, 0), (act1, 0), (act_s, 1), (dl3, 2), (dl2, 3), (zs, 3)):
        spans = geo.chunks(margin)
        lead, last = MARGIN + spans[0][0], MARGIN + sum(spans[-1])
        ref[:, :lead] = jnp.zeros((ref.shape[0], lead), ref.dtype)
        ref[:, last:] = jnp.zeros((ref.shape[0], geo.width - last), ref.dtype)
    place = lax.broadcasted_iota(jnp.int32, (8, geo.padded), 1).astype(F32)[:1]
    row = jnp.floor((place + 0.5) * (1.0 / pitch))
    col = place - row * pitch
    grow = row + (me_ch * rows - HALO).astype(F32)
    gcol = col + (me_t * cols - HALO).astype(F32)
    inside = (grow >= 0) & (grow < total_rows) & (gcol >= 0) & (gcol < total_cols) & (row < geo.high)
    mask = jnp.where(inside, 1.0, 0.0)
    mask_s[...] = jnp.broadcast_to(mask, mask_s.shape)
    rid = lax.broadcasted_iota(jnp.int32, (geo.high, geo.padded), 0).astype(F32)
    pick = jnp.sum(jnp.where(rid == row, pick_col, 0.0), axis=0, keepdims=True)
    offs = (2.0 * gcol - pick) * (1.0 / SIGMA)
    targ_s[...] = jnp.broadcast_to(jnp.exp(-0.5 * offs * offs), targ_s.shape)
    w2_f, w2_b, ws_f, ws_b, w3_f, w3_b = (value[...] for value in convs)
    head = jnp.broadcast_to(wh_ref[...].astype(F32), (8, wh_ref.shape[1]))
    head_col = head.T[:, :1]
    head_row = head.astype(BF16)
    srow = lax.broadcasted_iota(jnp.int32, (72, 9), 0)
    tapi = lax.broadcasted_iota(jnp.int32, (72, 9), 1)
    w1 = w1_ref[...]
    parts = []
    for a, b in PHASES:
        sel = jnp.zeros((72, 9), F32)
        for s, (sy, sx) in enumerate(SHIFTS):
            for p, (py, px) in enumerate(PHASES):
                ky, kx = 2 * sy + py - a + 1, 2 * sx + px - b + 1
                if 0 <= ky < 3 and 0 <= kx < 3:
                    sel = jnp.where((srow == 8 * s + p) & (tapi == 3 * ky + kx), 1.0, sel)
        parts.append(mm(sel.astype(BF16), w1))
    w1_b32 = jnp.concatenate(parts, axis=1)
    w1_f, w1_b = w1_b32.T.astype(BF16), w1_b32.astype(BF16)

    nat_h, nat_l = tables[0][...], tables[1][...]
    nat = (mm_nt(pb, nat_h) + mm_nt(pb, nat_l)) * scale
    filt_o[...] = nat[2 * HALO : 2 * HALO + 2 * rows].astype(BF16)
    x0[...] = jnp.zeros_like(x0)
    for b in range(2):
        t_h, t_l = tables[2 + 2 * b][...], tables[3 + 2 * b][...]
        un[:, :pitch] = (mm_nt(pb, t_h) + mm_nt(pb, t_l)) * scale
        for r in range(geo.high):
            at = MARGIN + r * pitch
            for a in range(2):
                x0[2 * a + b : 2 * a + b + 1, at : at + pitch] = un[2 * r + a : 2 * r + a + 1, :pitch]
    x0[:, MARGIN : MARGIN + geo.padded] = x0[:, MARGIN : MARGIN + geo.padded] * mask_s[...]

    for at, n in geo.chunks(0):
        patches = jnp.concatenate(
            [x0[:, MARGIN + at + geo.offset(*s) : MARGIN + at + geo.offset(*s) + n] for s in SHIFTS], axis=0
        ).astype(BF16)
        y, slope = silu_parts(mm(w1_f, patches))
        act1[:, MARGIN + at : MARGIN + at + n] = (y * mask_s[:1, at : at + n]).astype(BF16)
        sl1[:, at : at + n] = slope

    def fine_patches(ref, at, n):
        blocks = []
        for y, x in PATCH:
            p = 2 * (y % 2) + x % 2
            start = MARGIN + at + geo.offset(y // 2, x // 2)
            blocks.append(ref[p * f1 : (p + 1) * f1, start : start + n])
        return jnp.concatenate(blocks, axis=0)

    def coarse_patches(ref, at, n, sign):
        blocks = []
        for s in SHIFTS:
            start = MARGIN + at + sign * geo.offset(*s)
            blocks.append(ref[:, start : start + n])
        return jnp.concatenate(blocks, axis=0)

    for at, n in geo.chunks(1):
        y, slope = silu_parts(mm(w2_f, fine_patches(act1, at, n)))
        sl2[:, at : at + n] = slope
        y, slope = silu_parts(mm(ws_f, y.astype(BF16)))
        act_s[:, MARGIN + at : MARGIN + at + n] = (y * mask_s[:1, at : at + n]).astype(BF16)
        sls[:, at : at + n] = slope
    for at, n in geo.chunks(2):
        y, slope = silu_parts(mm(w3_f, coarse_patches(act_s, at, n, 1)))
        logits = mm(head_row, y.astype(BF16))
        log_s[:, at : at + n] = logits
        out = (0.5 * jnp.tanh(0.5 * logits) + 0.5 - targ_s[:, at : at + n]) * mask_s[:, at : at + n]
        dl3[:, MARGIN + at : MARGIN + at + n] = (head_col * out[:1] * slope).astype(BF16)
    for at, n in geo.chunks(3):
        back = mm(w3_b, coarse_patches(dl3, at, n, -1))
        back = mm(ws_b, (back * sls[:, at : at + n]).astype(BF16))
        dl2[:, MARGIN + at : MARGIN + at + n] = (
            back * sl2[:, at : at + n] * mask_s[:1, at : at + n]
        ).astype(BF16)
    for at, n in geo.chunks(3):
        back = mm(w2_b, fine_patches(dl2, at, n))
        delta = (back * sl1[:, at : at + n] * mask_s[:1, at : at + n]).astype(BF16)
        zs[:, MARGIN + at : MARGIN + at + n] = mm(w1_b, delta)
    for at, n in geo.chunks(4):
        total = None
        for s, shift in enumerate(SHIFTS):
            start = MARGIN + at - geo.offset(*shift)
            term = zs[8 * s : 8 * s + 8, start : start + n]
            total = term if total is None else total + term
        grad_s[:, at : at + n] = total
    for r in range(rows):
        at = (r + HALO) * pitch + HALO
        logit_o[r : r + 1, :] = log_s[:1, at : at + cols]
    spread = None
    lane = lax.broadcasted_iota(jnp.int32, (cols, 2 * cols), 1)
    sub = lax.broadcasted_iota(jnp.int32, (cols, 2 * cols), 0)
    for b in range(2):
        for r in range(rows):
            at = (r + HALO) * pitch + HALO
            for a in range(2):
                un[2 * r + a : 2 * r + a + 1, :cols] = grad_s[2 * a + b : 2 * a + b + 1, at : at + cols]
        g_h, g_l = split(un[: 2 * rows, :cols])
        place = jnp.where(lane == 2 * sub + b, 1.0, 0.0).astype(BF16)
        term = mm(g_h, place) + mm(g_l, place)
        spread = term if spread is None else spread + term
    grad_o[...] = spread


def unet_scratch(geo, f1, f2):
    return [
        pltpu.VMEM((8, geo.width), F32),
        pltpu.VMEM((8, geo.padded), F32),
        pltpu.VMEM((8, geo.padded), F32),
        pltpu.VMEM((4 * f1, geo.width), BF16),
        pltpu.VMEM((4 * f1, geo.padded), F32),
        pltpu.VMEM((4 * f1, geo.padded), F32),
        pltpu.VMEM((f2, geo.width), BF16),
        pltpu.VMEM((f2, geo.padded), F32),
        pltpu.VMEM((f2, geo.width), BF16),
        pltpu.VMEM((4 * f1, geo.width), BF16),
        pltpu.VMEM((72, geo.width), F32),
        pltpu.VMEM((8, geo.padded), F32),
        pltpu.VMEM((8, geo.padded), F32),
        pltpu.VMEM((2 * geo.high, -(-geo.pitch // 128) * 128), F32),
    ]


def out_shapes(geo):
    return (
        jax.ShapeDtypeStruct((2 * geo.rows, 2 * geo.cols), BF16),
        jax.ShapeDtypeStruct((geo.rows, geo.cols), F32),
        jax.ShapeDtypeStruct((2 * geo.rows, 2 * geo.cols), F32),
    )


def step_kernel(geo, samples, total_rows, freqs, pb, freq, pick, w1, w2, ws, w3, wh, *rest):
    me_ch, me_t = lax.axis_index("ch"), lax.axis_index("tm") * lax.axis_size("sub") + lax.axis_index("sub")
    tables = unet_tables(freq[...], freqs, me_t, geo, samples)
    unet(
        geo, samples, total_rows, pb[...], tables, pick[...], me_ch, me_t, w1, wh,
        conv_weights(w2, ws, w3), rest[:3], rest[3:],
    )


def exchange_kernel(geo, samples, *refs):
    hbm, outs, held = refs[:6], refs[6:23], refs[23:29]
    mine, landed, gath, sems_t, sems_c, sems_in = refs[29:]
    grp, ch, tm, sub = (lax.axis_index(name) for name in ("grp", "ch", "tm", "sub"))
    groups = lax.axis_size("ch")
    time_partners = [(tm, 1 - sub), (1 - tm, sub), (1 - tm, 1 - sub)]
    targets = [(grp, ch, t, s) for t, s in time_partners]
    targets += [(grp, lax.rem(ch + d, groups), tm, sub) for d in range(1, groups)]
    barrier = pltpu.get_barrier_semaphore()
    for target in targets:
        pl.semaphore_signal(barrier, inc=1, device_id=target, device_id_type=pl.DeviceIdType.MESH)
    loads = [pltpu.make_async_copy(a, b, sems_in.at[i]) for i, (a, b) in enumerate(zip(hbm, held))]
    for load in loads:
        load.start()
    record, freq, pick, w2, ws, w3 = held
    chans, times = record.shape
    freqs = freq.shape[1]
    half = chans // 2
    for load in loads[:3]:
        load.wait()
    freq_row = jnp.concatenate([freq[...], freq[...]], axis=1)
    first = (tm * 2 + sub) * times
    high, low = split(table(freq_row, freqs, first, 1, times, samples))
    part = mm(record[...], high) + mm(record[...], low)
    mine[...] = jnp.concatenate([part[:half], part[half:]], axis=1)
    pl.semaphore_wait(barrier, len(targets))
    copies = []
    for d in range(3):
        copies.append(
            pltpu.make_async_remote_copy(
                src_ref=mine,
                dst_ref=landed.at[d],
                send_sem=sems_t.at[0, d],
                recv_sem=sems_t.at[1, d],
                device_id=targets[d],
                device_id_type=pl.DeviceIdType.MESH,
            )
        )
        copies[-1].start()
    picks = jnp.broadcast_to(pick[...], (8, pick.shape[1])).astype(F32).T[:, :1]
    coarse = jnp.floor(picks * 0.125)
    side = jnp.concatenate([coarse, picks - 8.0 * coarse], axis=1)
    side = jnp.concatenate([side, jnp.zeros((half, 2 * freqs - 2), F32)], axis=1)
    side = jnp.concatenate([side, jnp.zeros_like(side)], axis=0)
    for load in loads[3:]:
        load.wait()
    for ref, value in zip(outs[1:7], conv_weights(w2, ws, w3)):
        ref[...] = value
    for copy in copies:
        copy.wait()
    total = (mine[...] + landed[0]) + (landed[1] + landed[2])
    spectrum = jnp.concatenate([total[:, : 2 * freqs], total[:, 2 * freqs :]], axis=0)
    gath[ch] = jnp.concatenate([spectrum, side], axis=1).astype(BF16)
    copies = []
    for d in range(1, groups):
        copies.append(
            pltpu.make_async_remote_copy(
                src_ref=gath.at[ch],
                dst_ref=gath.at[ch],
                send_sem=sems_c.at[0, d - 1],
                recv_sem=sems_c.at[1, d - 1],
                device_id=targets[2 + d],
                device_id_type=pl.DeviceIdType.MESH,
            )
        )
        copies[-1].start()
    outs[7][...], outs[8][...] = high, low
    for b in range(2):
        extended = split(table(freq_row, freqs, first - 2 * HALO + b, 2, geo.pitch, samples))
        outs[9 + 2 * b][...], outs[10 + 2 * b][...] = extended
    total_chans = groups * chans
    outs[13][...], outs[14][...] = dft_table(0, total_chans, total_chans)
    outs[15][...], outs[16][...] = dft_table(
        ch * chans - 2 * HALO + total_chans, chans + 4 * HALO, total_chans
    )
    for copy in copies:
        copy.wait()
    outs[0][...] = gath[...]


def exchange(geo, record, freq_bins, pick_index, w2, ws, w3, samples):
    groups = lax.axis_size("ch")
    chans = record.shape[0]
    freqs = freq_bins.shape[0]
    lanes = 4 * freqs
    f1, f2 = w2.shape[1], w3.shape[1]
    total = groups * chans
    args = (record, freq_bins[None], pick_index[None], w2, ws, w3)
    shapes = [(groups, chans, lanes), (4 * f1, 16 * f1), (4 * f1, 16 * f1), (f2, 4 * f1), (4 * f1, f2)]
    shapes += [(f2, 9 * f2)] * 2 + [(2 * geo.cols, 2 * freqs)] * 2 + [(geo.pitch, 2 * freqs)] * 4
    shapes += [(total, 2 * total)] * 2 + [(chans + 4 * HALO, 2 * total)] * 2
    vmem = pl.BlockSpec(memory_space=pltpu.VMEM)
    return pl.pallas_call(
        functools.partial(exchange_kernel, geo, samples),
        out_shape=tuple(pltpu.VMEM(shape, BF16) for shape in shapes),
        in_specs=[pl.BlockSpec(memory_space=pltpu.HBM)] * len(args),
        out_specs=(vmem,) * len(shapes),
        scratch_shapes=[pltpu.VMEM(arg.shape, arg.dtype) for arg in args]
        + [
            pltpu.VMEM((chans // 2, lanes), F32),
            pltpu.VMEM((3, chans // 2, lanes), F32),
            pltpu.VMEM((groups, chans, lanes), BF16),
            pltpu.SemaphoreType.DMA((2, 3)),
            pltpu.SemaphoreType.DMA((2, groups - 1)),
            pltpu.SemaphoreType.DMA((len(args),)),
        ],
        compiler_params=pltpu.CompilerParams(
            collective_id=0, has_side_effects=True
        ),
    )(*args)


def dft_table(first_row, rows, total):
    at = first_row + lax.broadcasted_iota(jnp.int32, (rows, 2 * total), 0)
    lane = lax.broadcasted_iota(jnp.int32, (rows, 2 * total), 1)
    quarter = jnp.where(lane >= total, 3 * total // 4, 0)
    return split(cosine_turns((at * (lane & (total - 1)) + quarter) & (total - 1), total))


def small_kernel(geo, samples, freqs, limit, w1, wh, gath, *rest):
    convs, tables, dfts, rest = rest[:6], rest[6:12], rest[12:16], rest[16:]
    me_ch, me_t = lax.axis_index("ch"), lax.axis_index("tm") * lax.axis_size("sub") + lax.axis_index("sub")
    groups, chans, _ = gath.shape
    total = groups * chans
    both = 2 * freqs
    spec = jnp.concatenate([gath[g].astype(F32) for g in range(groups)], axis=0)
    re, im = spec[:, :freqs], spec[:, freqs:both]
    stack = jnp.concatenate(
        [jnp.concatenate([re, im], axis=1), jnp.concatenate([im, -re], axis=1)], axis=0
    ).astype(BF16)
    high, low = dfts[0][...], dfts[1][...]
    wave = mm(high, stack) + mm(low, stack)
    index = lax.broadcasted_iota(jnp.int32, (total, both), 0)
    limits = jnp.concatenate([limit[...], limit[...]], axis=1)
    wave = jnp.where(jnp.minimum(index, total - index) <= limits, wave, 0.0)
    re, im = wave[:, :freqs], wave[:, freqs:]
    stack_h, stack_l = split(jnp.concatenate([wave, jnp.concatenate([-im, re], axis=1)], axis=0))
    high, low = dfts[2][...], dfts[3][...]
    pb = (mm(high, stack_h) + mm(low, stack_h) + mm(high, stack_l)) * (1.0 / total)
    around = [jnp.maximum(me_ch - 1, 0), me_ch, jnp.minimum(me_ch + 1, groups - 1)]
    rows = geo.rows
    picks = []
    for g, (first, last) in zip(around, ((rows - HALO, rows), (0, rows), (0, HALO))):
        side = gath[g].astype(F32)[first:last]
        picks.append(side[:, both : both + 1] * 8.0 + side[:, both + 1 : both + 2])
    pick_col = jnp.concatenate(picks, axis=0)
    unet(
        geo, samples, total // 2, pb.astype(BF16), tables, pick_col, me_ch, me_t, w1, wh,
        convs, rest[:3], rest[3:],
    )


def wave_tables(total):
    index = jnp.arange(total, dtype=jnp.int32)
    angle = (index[:, None] * index[None, :] % total).astype(F32) * (2.0 * math.pi / total)
    return jnp.cos(angle), jnp.sin(angle)


def spectral_wide(record, freq_bins, wave_limit, geo, samples, total_chans):
    precise = lax.Precision.HIGHEST
    local_chans, local_times = record.shape
    chan_groups = lax.axis_size("ch")
    time_groups = lax.axis_size(("tm", "sub"))
    freq_count = freq_bins.shape[0]
    bins_local = freq_count // (chan_groups * time_groups)
    time_index = lax.axis_index(("tm", "sub")) * local_times + jnp.arange(local_times, dtype=jnp.int32)
    angle = (freq_bins[:, None] * time_index[None, :] % samples).astype(F32) * (2.0 * math.pi / samples)
    signal = record.astype(F32)
    real_part = jnp.einsum("ft,ct->fc", jnp.cos(angle), signal, precision=precise)
    imag_part = -jnp.einsum("ft,ct->fc", jnp.sin(angle), signal, precision=precise)
    summed = lax.psum_scatter(
        jnp.concatenate([real_part, imag_part], axis=1), ("tm", "sub"), scatter_dimension=0, tiled=True
    )
    gathered = lax.all_to_all(summed.astype(BF16), "ch", split_axis=0, concat_axis=1, tiled=True)
    block = lax.axis_index(("tm", "sub")) * chan_groups + lax.axis_index("ch")
    arranged = gathered.reshape(bins_local, chan_groups, 2, local_chans).transpose(2, 0, 1, 3)
    arranged = arranged.reshape(2, bins_local, total_chans).astype(F32)
    limits = lax.dynamic_slice_in_dim(wave_limit, block * bins_local, bins_local)
    cosine, sine = wave_tables(total_chans)
    dot = functools.partial(jnp.dot, precision=precise)
    re = dot(arranged[0], cosine) + dot(arranged[1], sine)
    im = dot(arranged[1], cosine) - dot(arranged[0], sine)
    index = jnp.arange(total_chans, dtype=jnp.int32)
    passing = jnp.minimum(index, total_chans - index)[None] <= limits[:, None]
    re, im = jnp.where(passing, re, 0.0), jnp.where(passing, im, 0.0)
    out = jnp.stack([dot(re, cosine) - dot(im, sine), dot(im, cosine) + dot(re, sine)]) / total_chans
    out = jnp.pad(out.astype(BF16), ((0, 0), (0, 0), (2 * HALO, 2 * HALO)))
    wide = local_chans + 4 * HALO
    outgoing = jnp.stack([out[:, :, g * local_chans : g * local_chans + wide] for g in range(chan_groups)])
    outgoing = outgoing.transpose(2, 0, 1, 3).reshape(bins_local, chan_groups * 2 * wide)
    returned = lax.all_to_all(outgoing, "ch", split_axis=1, concat_axis=0, tiled=True)
    values = lax.all_gather(returned, ("tm", "sub"), axis=0, tiled=True)
    return values.reshape(freq_count, 2, wide).transpose(2, 1, 0).reshape(wide, 2 * freq_count)


def local(record, freq_bins, wave_limit, pick_index, w1, w2, ws, w3, wh):
    local_chans, local_times = record.shape
    chan_groups = lax.axis_size("ch")
    samples = local_times * lax.axis_size(("tm", "sub"))
    total_chans = local_chans * chan_groups
    freqs = freq_bins.shape[0]
    geo = Geometry(local_chans // 2, local_times // 2)
    vmem = pl.BlockSpec(memory_space=pltpu.VMEM)
    call = dict(
        out_shape=out_shapes(geo),
        out_specs=(vmem,) * 3,
        scratch_shapes=unet_scratch(geo, w2.shape[1], w3.shape[1]),
        compiler_params=pltpu.CompilerParams(vmem_limit_bytes=48 * 2**20),
    )
    if lax.axis_size("tm") == 2 and lax.axis_size("sub") == 2 and freqs == 32 and total_chans <= 256:
        ready = exchange(
            geo, record, freq_bins, pick_index, w2, jnp.swapaxes(ws, 1, 2), w3, samples
        )
        args = (wave_limit[None], w1, wh[None], *ready)
        return pl.pallas_call(
            functools.partial(small_kernel, geo, samples, freqs), in_specs=[vmem] * len(args), **call
        )(*args)
    pb = spectral_wide(record, freq_bins, wave_limit, geo, samples, total_chans)
    freq_row = jnp.concatenate([freq_bins, freq_bins])[None]
    picks = jnp.pad(lax.all_gather(pick_index, "ch", axis=0, tiled=True), (HALO, HALO))
    picks = lax.dynamic_slice_in_dim(picks, lax.axis_index("ch") * geo.rows, geo.high)
    return pl.pallas_call(
        functools.partial(step_kernel, geo, samples, total_chans // 2, freqs),
        in_specs=[vmem] * 8,
        **call,
    )(pb, freq_row, picks.astype(F32)[:, None], w1, w2, jnp.swapaxes(ws, 1, 2), w3, wh[None])


def solution(mesh):
    return jax.shard_map(
        local,
        mesh=mesh,
        in_specs=(
            P(("grp", "ch"), ("tm", "sub")),
            P("grp"),
            P("grp"),
            P(("grp", "ch")),
            P(),
            P(),
            P(),
            P(),
            P(),
        ),
        out_specs=(P(("grp", "ch"), ("tm", "sub")),) * 3,
        check_vma=False,
    )
```
